32 devices in a mesh: fsdp: 8 (over z, x), ctx: 4 (over y, core).
Axes of the slice: x: 2, y: 2, z: 4, core: 2. Of those that a mesh axis runs over, the one named last changes fastest.
Arguments:
- tokens: bfloat16 [64, 1024, 576], P('fsdp', 'ctx'), may hold values from -6 to 6
- segments: int32 [64, 1024], P('fsdp', 'ctx'), may hold values from 0 to 7, as said below
- positions: int32 [64, 1024], P('fsdp', 'ctx'), may hold values from 0 to 1023, as said below
- query_weight: bfloat16 [576, 576], P('fsdp'), may hold values from -0.25 to 0.25
- key_weight: bfloat16 [576, 192], P('fsdp'), may hold values from -0.25 to 0.25
- value_weight: bfloat16 [576, 192], P('fsdp'), may hold values from -0.25 to 0.25
- output_weight: bfloat16 [576, 576], P('fsdp'), may hold values from -1 to 1
- gate_weight: bfloat16 [576, 1536], P('fsdp'), may hold values from -0.25 to 0.25
- up_weight: bfloat16 [576, 1536], P('fsdp'), may hold values from -0.25 to 0.25
- down_weight: bfloat16 [1536, 576], P('fsdp'), may hold values from -0.15625 to 0.15625
- attn_gain: bfloat16 [576], P('fsdp'), may hold values from 0.5 to 1.5
- ffn_gain: bfloat16 [576], P('fsdp'), may hold values from 0.5 to 1.5
- cotangent: bfloat16 [64, 1024, 576], P('fsdp', 'ctx'), may hold values from -6 to 6
Outputs:
- block_out: bfloat16 [64, 1024, 576], P('fsdp', 'ctx')
- grad_tokens: bfloat16 [64, 1024, 576], P('fsdp', 'ctx')
- grad_query: float32 [576, 576], P('fsdp')
- grad_key: float32 [576, 192], P('fsdp')
- grad_value: float32 [576, 192], P('fsdp')
- grad_output: float32 [576, 576], P('fsdp')
- grad_gate: float32 [576, 1536], P('fsdp')
- grad_up: float32 [576, 1536], P('fsdp')
- grad_down: float32 [1536, 576], P('fsdp')
- grad_attn_gain: float32 [576], P('fsdp')
- grad_ffn_gain: float32 [576], P('fsdp')
The draws below stay inside these ranges and needn't reach their ends.
Inputs may be any that keep to these rules, and one draw needn't show every extreme that they name: `segments`: along each packed sequence the document numbers start at 0 and rise by one at each new document. In every group of 8 sequences that share an index of fsdp, one sequence is a single document and another reaches the largest document number. `positions`: each token's position counts the tokens before it in its own document.
All inputs are finite; a program needn't handle non-finite values.
Results may differ from the reference program's by a relative error of at most 0.02.
Values may be sent and summed in bfloat16 or wider, within the bound.
A program may use at most 192 MiB of HBM per device.

```python
import math
import jax
import jax.numpy as jnp
from jax import lax

D = 576
HEADS = 9
KV_HEADS = 3
HEAD_DIM = 64
FF = 1536
LEN = 1024
SEQS = 8
SEQUENCES = 64


def boundaries(key):
    starts = jax.random.randint(jax.random.fold_in(key, 11), (SEQUENCES, LEN), 0, max(LEN // 6, 2)) == 0
    group_count = SEQUENCES // SEQS
    chosen = jax.random.randint(jax.random.fold_in(key, 12), (group_count,), 0, SEQS)
    offset = jax.random.randint(jax.random.fold_in(key, 13), (group_count,), 1, SEQS)
    busy = (chosen + offset) % SEQS
    row_index = jnp.arange(SEQUENCES, dtype=jnp.int32)
    single = row_index % SEQS == chosen[row_index // SEQS]
    crowded = row_index % SEQS == busy[row_index // SEQS]
    columns = jnp.arange(LEN, dtype=jnp.int32)
    regular = columns % (LEN // 8) == 0
    flags = (starts | crowded[:, None] & regular[None, :]) & jnp.logical_not(single)[:, None] & (columns[None, :] > 0)
    counted = jnp.cumsum(flags.astype(jnp.int32), axis=1)
    return flags & (counted <= 7)


def draw_segments(key, part):
    flags = boundaries(key)
    return jnp.cumsum(flags.astype(jnp.int32), axis=1).astype(jnp.int32)


def draw_positions(key, part):
    flags = boundaries(key)
    places = jnp.broadcast_to(jnp.arange(LEN, dtype=jnp.int32)[None, :], (SEQUENCES, LEN))
    starting = lax.cummax(jnp.where(flags, places, 0), axis=1)
    return (places - starting).astype(jnp.int32)


def level_of(key, shape, pieces, low, largest):
    loudness = 1.0
    for dim, parts in pieces:
        draws = jax.random.uniform(jax.random.fold_in(jax.random.fold_in(key, 6), dim), (parts,), jnp.float32, low / len(pieces), largest / len(pieces))
        loudness = loudness * jnp.repeat(jnp.exp(draws), shape[dim] // parts).reshape((-1,) + (1,) * (len(shape) - 1 - dim))
    return loudness


def centred(stream_key, shape, spread, bound, split=(), kind=jnp.bfloat16):
    values = spread * jax.random.normal(stream_key, shape, jnp.float32)
    if split:
        values = values * level_of(stream_key, shape, split, -0.22, 0.18)
    return jnp.clip(values, -bound, bound).astype(kind)


def setup_inputs(seed: int = 0) -> dict:
    streams_of = jax.random.split(jax.random.key(seed), 14)
    tokens = centred(streams_of[0], (SEQUENCES, LEN, D), 1.0, 6.0, ((0, 8), (1, 4)))
    segments = draw_segments(jax.random.fold_in(streams_of[13], 71), 0)
    positions = draw_positions(jax.random.fold_in(streams_of[13], 71), 0)
    query_weight = centred(streams_of[3], (D, D), D ** -0.5, 0.25, ((0, 8),))
    key_weight = centred(streams_of[4], (D, KV_HEADS * HEAD_DIM), D ** -0.5, 0.25, ((0, 8),))
    value_weight = centred(streams_of[5], (D, KV_HEADS * HEAD_DIM), D ** -0.5, 0.25, ((0, 8),))
    output_weight = centred(streams_of[6], (D, D), (D // 16) ** -0.5, 1.0, ((0, 8),))
    gate_weight = centred(streams_of[7], (D, FF), D ** -0.5, 0.25, ((0, 8),))
    up_weight = centred(streams_of[8], (D, FF), D ** -0.5, 0.25, ((0, 8),))
    down_weight = centred(streams_of[9], (FF, D), FF ** -0.5, 0.15625, ((0, 8),))
    attn_gain = jnp.clip(1.0 + 0.1 * jax.random.normal(streams_of[10], (D,), jnp.float32), 0.5, 1.5).astype(jnp.bfloat16)
    ffn_gain = jnp.clip(1.0 + 0.1 * jax.random.normal(streams_of[11], (D,), jnp.float32), 0.5, 1.5).astype(jnp.bfloat16)
    cotangent = centred(streams_of[12], (SEQUENCES, LEN, D), 1.0, 6.0, ((0, 8), (1, 4)))
    return {"tokens": tokens, "segments": segments, "positions": positions, "query_weight": query_weight, "key_weight": key_weight, "value_weight": value_weight, "output_weight": output_weight, "gate_weight": gate_weight, "up_weight": up_weight, "down_weight": down_weight, "attn_gain": attn_gain, "ffn_gain": ffn_gain, "cotangent": cotangent}


epsilon = 1e-05
rope_base = 100000.0
masked_value = -1e+30

@jax.custom_vjp
def low(v):
    return lax.optimization_barrier(v.astype(jnp.bfloat16)).astype(jnp.float32)

@jax.custom_vjp
def low_back(v):
    return v

def low_keep(v):
    return (low(v), None)

def low_pass(kept, grad):
    return (grad,)

def back_keep(v):
    return (v, None)

def back_low(kept, grad):
    return (low(grad),)
low.defvjp(low_keep, low_pass)
low_back.defvjp(back_keep, back_low)

def tables(places):
    half_dim = HEAD_DIM // 2
    frequency = rope_base ** (-(jnp.arange(half_dim, dtype=jnp.float32) * (2.0 / HEAD_DIM)))
    angles = places.astype(jnp.float32)[..., None] * frequency
    return (jnp.cos(angles), jnp.sin(angles))

def rotate(values, cosine, sine):
    half_dim = HEAD_DIM // 2
    front_half = values[..., :half_dim]
    back_half = values[..., half_dim:]
    cos_wide = cosine[..., None, :]
    sin_wide = sine[..., None, :]
    return jnp.concatenate([front_half * cos_wide - back_half * sin_wide, back_half * cos_wide + front_half * sin_wide], axis=-1)

def normalize(values, gain_row):
    return values * lax.rsqrt(lax.optimization_barrier(jnp.mean(values * values, axis=-1, keepdims=True)) + epsilon) * gain_row

def project(values, matrix):
    return jnp.einsum('bld,de->ble', values, matrix, precision=lax.Precision.HIGHEST)

def layer(inputs, params, segments, positions):
    query_weight, key_weight, value_weight, output_weight, gate_weight, up_weight, down_weight, attn_gain, ffn_gain = params
    seq_batch = inputs.shape[0]
    group_size = HEADS // KV_HEADS
    normed_one = low(normalize(inputs, attn_gain))
    query_pre = low_back(project(normed_one, query_weight))
    key_pre = low_back(project(normed_one, key_weight))
    value_pre = low_back(project(normed_one, value_weight))
    cosine, sine = tables(positions)
    queries = low(rotate(query_pre.reshape(seq_batch, LEN, HEADS, HEAD_DIM), cosine, sine))
    key_rows = low(rotate(key_pre.reshape(seq_batch, LEN, KV_HEADS, HEAD_DIM), cosine, sine))
    value_rows = low(value_pre.reshape(seq_batch, LEN, KV_HEADS, HEAD_DIM))
    grouped = queries.reshape(seq_batch, LEN, KV_HEADS, group_size, HEAD_DIM)
    raw_scores = jnp.einsum('bqkgd,bnkd->bkgqn', grouped, key_rows, precision=lax.Precision.HIGHEST) * (1.0 / math.sqrt(HEAD_DIM))
    places = jnp.arange(LEN, dtype=jnp.int32)
    allowed = (segments[:, :, None] == segments[:, None, :]) & (places[:, None] >= places[None, :])
    scores = low_back(jnp.where(allowed[:, None, None], raw_scores, masked_value))
    maxima = lax.optimization_barrier(jnp.max(scores, axis=-1, keepdims=True))
    exponent = jnp.exp(scores - maxima)
    attn_probs = low(exponent / lax.optimization_barrier(jnp.sum(exponent, axis=-1, keepdims=True)))
    mixed_heads = jnp.einsum('bkgqn,bnkd->bqkgd', attn_probs, value_rows, precision=lax.Precision.HIGHEST)
    mixed_heads = low(low_back(mixed_heads.reshape(seq_batch, LEN, HEADS * HEAD_DIM)))
    middle = inputs + low_back(project(mixed_heads, output_weight))
    normed_two = low(normalize(middle, ffn_gain))
    gate_pre = low_back(project(normed_two, gate_weight))
    up_pre = low_back(project(normed_two, up_weight))
    hidden = low(gate_pre * jax.nn.sigmoid(gate_pre) * up_pre)
    return middle + low_back(project(hidden, down_weight))

def reference(tokens, segments, positions, query_weight, key_weight, value_weight, output_weight, gate_weight, up_weight, down_weight, attn_gain, ffn_gain, cotangent):
    params = tuple((item.astype(jnp.float32) for item in (query_weight, key_weight, value_weight, output_weight, gate_weight, up_weight, down_weight, attn_gain, ffn_gain)))
    block_count = tokens.shape[0] // 4
    token_blocks = tokens.astype(jnp.float32).reshape(block_count, 4, LEN, D)
    cot_blocks = cotangent.astype(jnp.float32).reshape(block_count, 4, LEN, D)
    seg_blocks = segments.reshape(block_count, 4, LEN)
    pos_blocks = positions.reshape(block_count, 4, LEN)

    def scan_step(running, block_data):
        data_block, seg_block, pos_block, cot_block = block_data

        def apply_layer(data_in, param_in):
            return layer(data_in, param_in, seg_block, pos_block)
        result, pullback = jax.vjp(apply_layer, data_block, params)
        grad_data, grad_params = pullback(cot_block)
        running = jax.tree.map(lambda left, right: left + right, running, grad_params)
        return (running, (result.astype(jnp.bfloat16), grad_data.astype(jnp.bfloat16)))
    zero_grads = jax.tree.map(jnp.zeros_like, params)
    running, (results, grad_datas) = lax.scan(scan_step, zero_grads, (token_blocks, seg_blocks, pos_blocks, cot_blocks))
    return (results.reshape(tokens.shape), grad_datas.reshape(tokens.shape), running[0], running[1], running[2], running[3], running[4], running[5], running[6], running[7], running[8])
```

```python
import functools
import math

import jax
import jax.numpy as jnp
from jax import lax
from jax.experimental import pallas as pl
from jax.experimental.pallas import tpu as pltpu
from jax.sharding import PartitionSpec as P

HEADS = 9
KV_HEADS = 3
HEAD_DIM = 64


epsilon = 1e-05
rope_base = 100000.0
masked_value = -1e30


def tables(places):
    half_dim = HEAD_DIM // 2
    frequency = rope_base ** (-(jnp.arange(half_dim, dtype=jnp.float32) * (2.0 / HEAD_DIM)))
    angles = frequency[:, None] * places.astype(jnp.float32)[None, :]
    return (jnp.cos(angles), jnp.sin(angles))


def rotate(values, cosine, sine, heads):
    half_dim = HEAD_DIM // 2
    halves = values.reshape(heads, 2, half_dim, -1)
    front = halves[:, 0]
    back = halves[:, 1]
    return jnp.stack(
        [front * cosine - back * sine, back * cosine + front * sine], axis=1
    ).reshape(heads * HEAD_DIM, -1)


def normalize_parts(values):
    inverse = lax.rsqrt(jnp.mean(values * values, axis=-1, keepdims=True) + epsilon)
    return (values * inverse, inverse)


def norm_back(grad_normed, scaled, inverse, gain_row):
    grad_scaled = grad_normed * gain_row
    return inverse * (grad_scaled - scaled * jnp.mean(grad_scaled * scaled, axis=-1, keepdims=True))


def forward_dot(left, right):
    return jnp.dot(left, right, preferred_element_type=jnp.float32)


def contract_rows(left, right):
    return lax.dot_general(
        left, right, (((0,), (0,)), ((), ())), preferred_element_type=jnp.float32
    )


def times_transposed(left, right):
    return lax.dot_general(
        left, right, (((1,), (1,)), ((), ())), preferred_element_type=jnp.float32
    )


def dot_tn(left, right):
    return lax.dot_general(
        left, right, (((0,), (0,)), ((), ())), preferred_element_type=jnp.float32
    )


def fill_bias(bias, row_ref, column_ref, block):
    length = bias.shape[0]
    for begin in range(0, length, block):
        end = begin + block
        keys = lax.broadcasted_iota(jnp.int32, (end, block), 0)
        places = lax.broadcasted_iota(jnp.int32, (end, block), 1) + begin
        same = column_ref[:end, :1] == row_ref[0, :, begin:end]
        bias[:end, begin:end] = jnp.where(same & (keys <= places), 0.0, masked_value)


def attend_kernel(block, q_ref, k_ref, v_ref, row_ref, column_ref, mixed_ref, total_ref, bias):
    @pl.when(pl.program_id(1) == 0)
    def _():
        fill_bias(bias, row_ref, column_ref, block)

    length = bias.shape[0]
    for begin in range(0, length, block):
        end = begin + block
        scores = dot_tn(k_ref[:, :end], q_ref[:, begin:end]) + bias[:end, begin:end]
        maxima = jnp.max(scores, axis=0, keepdims=True)
        exponent = jnp.exp(scores - maxima)
        totals = jnp.sum(exponent, axis=0, keepdims=True)
        mixed = jnp.dot(
            v_ref[:, :end], exponent.astype(jnp.bfloat16), preferred_element_type=jnp.float32
        )
        mixed_ref[:, begin:end] = (mixed / totals).astype(jnp.bfloat16)
        total_ref[0, 0, :, begin:end] = maxima + jnp.log(totals)


def rotate_back(values, cosine, sine):
    half_dim = HEAD_DIM // 2
    front = values[:half_dim]
    back = values[half_dim:]
    return jnp.concatenate([front * cosine + back * sine, back * cosine - front * sine], axis=0)


def attend_back_kernel(
    block,
    group,
    q_ref,
    k_ref,
    v_ref,
    grad_ref,
    mixed_ref,
    total_ref,
    row_ref,
    column_ref,
    cos_ref,
    sin_ref,
    dq_ref,
    dk_ref,
    dv_ref,
    bias,
    dk_sum,
    dv_sum,
):
    head = pl.program_id(1)

    @pl.when(head == 0)
    def _():
        fill_bias(bias, row_ref, column_ref, block)

    @pl.when(head % group == 0)
    def _():
        dk_sum[...] = jnp.zeros_like(dk_sum)
        dv_sum[...] = jnp.zeros_like(dv_sum)

    length = bias.shape[0]
    score_scale = 1.0 / math.sqrt(HEAD_DIM)
    for begin in range(0, length, block):
        end = begin + block
        query = q_ref[:, begin:end]
        grad = grad_ref[:, begin:end]
        centre = jnp.sum(
            grad.astype(jnp.float32) * mixed_ref[:, begin:end].astype(jnp.float32),
            axis=0,
            keepdims=True,
        )
        keys = k_ref[:, :end]
        scores = dot_tn(keys, query) + bias[:end, begin:end]
        probs = jnp.exp(scores - total_ref[0, 0, :, begin:end])
        grad_probs = dot_tn(v_ref[:, :end], grad)
        grad_scores = (probs * (grad_probs - centre)).astype(jnp.bfloat16)
        dv_sum[:, :end] += times_transposed(grad, probs.astype(jnp.bfloat16))
        dk_sum[:, :end] += times_transposed(query, grad_scores)
        dq = jnp.dot(keys, grad_scores, preferred_element_type=jnp.float32) * score_scale
        dq_ref[:, begin:end] = rotate_back(
            dq, cos_ref[:, begin:end], sin_ref[:, begin:end]
        ).astype(jnp.bfloat16)

    @pl.when(head % group == group - 1)
    def _():
        dk_ref[...] = rotate_back(dk_sum[...], cos_ref[...], sin_ref[...]).astype(jnp.bfloat16)
        dv_ref[...] = dv_sum[...].astype(jnp.bfloat16)


VMEM_LIMIT = 48 * 1024 * 1024


def specs(length, group):
    per_head = pl.BlockSpec((HEAD_DIM, length), lambda s, h: (h, s))
    per_key = pl.BlockSpec((HEAD_DIM, length), lambda s, h: (h // group, s))
    total = pl.BlockSpec((1, 1, 1, length), lambda s, h: (s, h, 0, 0))
    row = pl.BlockSpec((1, 1, length), lambda s, h: (s, 0, 0))
    column = pl.BlockSpec((length, 1), lambda s, h: (s, 0))
    table = pl.BlockSpec((HEAD_DIM // 2, length), lambda s, h: (0, s))
    return per_head, per_key, total, row, column, table


def attend(queries, keys, values, seg_row, seg_column, sequences, length):
    group = HEADS // KV_HEADS
    block = min(256, length)
    per_head, per_key, total, row, column, _ = specs(length, group)
    rows = sequences * length
    area = sequences * HEADS * length * (length + block) // 2
    return pl.pallas_call(
        functools.partial(attend_kernel, block),
        grid=(sequences, HEADS),
        in_specs=[per_head, per_key, per_key, row, column],
        out_specs=[per_head, total],
        out_shape=[
            jax.ShapeDtypeStruct((HEADS * HEAD_DIM, rows), jnp.bfloat16),
            jax.ShapeDtypeStruct((sequences, HEADS, 1, length), jnp.float32),
        ],
        scratch_shapes=[pltpu.VMEM((length, length), jnp.float32)],
        compiler_params=pltpu.CompilerParams(vmem_limit_bytes=VMEM_LIMIT),
        cost_estimate=pl.CostEstimate(
            flops=area * HEAD_DIM * 16, bytes_accessed=rows * 4096, transcendentals=area
        ),
        name="attend",
    )(queries, keys, values, seg_row, seg_column)


def attend_back(
    queries, keys, values, grads, mixed, totals, seg_row, seg_column, cosine, sine, sequences, length
):
    group = HEADS // KV_HEADS
    block = min(256, length)
    per_head, per_key, total, row, column, table = specs(length, group)
    rows = sequences * length
    area = sequences * HEADS * length * (length + block) // 2
    return pl.pallas_call(
        functools.partial(attend_back_kernel, block, group),
        grid=(sequences, HEADS),
        in_specs=[
            per_head,
            per_key,
            per_key,
            per_head,
            per_head,
            total,
            row,
            column,
            table,
            table,
        ],
        out_specs=[per_head, per_key, per_key],
        out_shape=[
            jax.ShapeDtypeStruct((HEADS * HEAD_DIM, rows), jnp.bfloat16),
            jax.ShapeDtypeStruct((KV_HEADS * HEAD_DIM, rows), jnp.bfloat16),
            jax.ShapeDtypeStruct((KV_HEADS * HEAD_DIM, rows), jnp.bfloat16),
        ],
        scratch_shapes=[
            pltpu.VMEM((length, length), jnp.float32),
            pltpu.VMEM((HEAD_DIM, length), jnp.float32),
            pltpu.VMEM((HEAD_DIM, length), jnp.float32),
        ],
        compiler_params=pltpu.CompilerParams(vmem_limit_bytes=VMEM_LIMIT),
        cost_estimate=pl.CostEstimate(
            flops=area * HEAD_DIM * 40, bytes_accessed=rows * 8192, transcendentals=area
        ),
        name="attend_back",
    )(queries, keys, values, grads, mixed, totals, seg_row, seg_column, cosine, sine)


def local(
    tokens,
    segments,
    positions,
    query_weight,
    key_weight,
    value_weight,
    output_weight,
    gate_weight,
    up_weight,
    down_weight,
    attn_gain,
    ffn_gain,
    cotangent,
):
    def enter(values):
        return lax.all_to_all(values, "ctx", split_axis=0, concat_axis=1, tiled=True)

    def leave(values):
        return lax.all_to_all(values, "ctx", split_axis=1, concat_axis=0, tiled=True)

    tokens = enter(tokens)
    places = enter(jnp.stack([segments, positions], axis=-1))
    segments = places[..., 0]
    positions = places[..., 1]
    cotangent = enter(cotangent)
    seq_count, full_len, model_width = tokens.shape
    row_count = seq_count * full_len
    score_scale = 1.0 / math.sqrt(HEAD_DIM)
    shards = (
        query_weight,
        key_weight,
        value_weight,
        output_weight,
        gate_weight,
        up_weight,
        down_weight,
        attn_gain,
        ffn_gain,
    )
    (
        full_query,
        full_key,
        full_value,
        full_output,
        full_gate,
        full_up,
        full_down,
        full_attn,
        full_ffn,
    ) = (
        lax.all_gather(shards[0], "fsdp", axis=0, tiled=True),
        lax.all_gather(shards[1], "fsdp", axis=0, tiled=True),
        lax.all_gather(shards[2], "fsdp", axis=0, tiled=True),
        lax.all_gather(shards[3], "fsdp", axis=0, tiled=True),
        lax.all_gather(shards[4], "fsdp", axis=0, tiled=True),
        lax.all_gather(shards[5], "fsdp", axis=0, tiled=True),
        lax.all_gather(shards[6], "fsdp", axis=0, tiled=True),
        lax.all_gather(shards[7], "fsdp", axis=0, tiled=True),
        lax.all_gather(shards[8], "fsdp", axis=0, tiled=True),
    )
    attn_scale = full_attn.astype(jnp.float32)
    ffn_scale = full_ffn.astype(jnp.float32)
    inputs = tokens.astype(jnp.float32).reshape(row_count, model_width)
    scaled_one, inverse_one = normalize_parts(inputs)
    normed_one = (scaled_one * attn_scale).astype(jnp.bfloat16)
    def features(weight, rows):
        return lax.dot_general(
            weight, rows, (((0,), (1,)), ((), ())), preferred_element_type=jnp.float32
        )

    cosine, sine = tables(positions.reshape(row_count))
    queries = (rotate(features(full_query, normed_one), cosine, sine, HEADS) * score_scale).astype(
        jnp.bfloat16
    )
    key_rows = rotate(features(full_key, normed_one), cosine, sine, KV_HEADS).astype(jnp.bfloat16)
    value_rows = features(full_value, normed_one).astype(jnp.bfloat16)
    seg_row = segments.reshape(seq_count, 1, full_len)
    seg_column = segments.reshape(row_count, 1)
    mixed_rows, log_totals = attend(
        queries, key_rows, value_rows, seg_row, seg_column, seq_count, full_len
    )
    middle = inputs + dot_tn(mixed_rows, full_output)
    scaled_two, inverse_two = normalize_parts(middle)
    normed_two = (scaled_two * ffn_scale).astype(jnp.bfloat16)
    gate_pre = forward_dot(normed_two, full_gate)
    up_pre = forward_dot(normed_two, full_up)
    sigmoid_gate = jax.nn.sigmoid(gate_pre)
    silu_gate = gate_pre * sigmoid_gate
    hidden = (silu_gate * up_pre).astype(jnp.bfloat16)
    block_out = leave(
        (middle + forward_dot(hidden, full_down)).astype(jnp.bfloat16).reshape(tokens.shape)
    )
    grad_rows = cotangent.astype(jnp.float32).reshape(row_count, model_width)
    grad_low = grad_rows.astype(jnp.bfloat16)
    grad_down = contract_rows(hidden, grad_low)
    grad_hidden = times_transposed(grad_low, full_down)
    grad_up_in = (grad_hidden * silu_gate).astype(jnp.bfloat16)
    grad_gate_in = (
        grad_hidden * up_pre * sigmoid_gate * (1.0 + gate_pre * (1.0 - sigmoid_gate))
    ).astype(jnp.bfloat16)
    grad_gate = contract_rows(normed_two, grad_gate_in)
    grad_up = contract_rows(normed_two, grad_up_in)
    grad_normed_two = times_transposed(grad_gate_in, full_gate) + times_transposed(
        grad_up_in, full_up
    )
    grad_ffn = jnp.sum(grad_normed_two * scaled_two, axis=0)
    grad_middle = grad_rows + norm_back(grad_normed_two, scaled_two, inverse_two, ffn_scale)
    grad_branch = grad_middle.astype(jnp.bfloat16)
    grad_output = forward_dot(mixed_rows, grad_branch)
    grad_mixed = times_transposed(full_output, grad_branch).astype(jnp.bfloat16)
    grad_query_in, grad_key_in, grad_value_in = attend_back(
        queries,
        key_rows,
        value_rows,
        grad_mixed,
        mixed_rows,
        log_totals,
        seg_row,
        seg_column,
        cosine,
        sine,
        seq_count,
        full_len,
    )

    def weight_grad(grads):
        return lax.dot_general(
            normed_one, grads, (((0,), (1,)), ((), ())), preferred_element_type=jnp.float32
        )

    def row_grad(grads, weight):
        return lax.dot_general(
            grads, weight, (((0,), (1,)), ((), ())), preferred_element_type=jnp.float32
        )

    grad_query = weight_grad(grad_query_in)
    grad_key = weight_grad(grad_key_in)
    grad_value = weight_grad(grad_value_in)
    grad_normed_one = (
        row_grad(grad_query_in, full_query)
        + row_grad(grad_key_in, full_key)
        + row_grad(grad_value_in, full_value)
    )
    grad_attn = jnp.sum(grad_normed_one * scaled_one, axis=0)
    grad_tokens = leave(
        (grad_middle + norm_back(grad_normed_one, scaled_one, inverse_one, attn_scale))
        .astype(jnp.bfloat16)
        .reshape(tokens.shape)
    )
    owned = (
        lax.psum_scatter(
            grad_query.astype(jnp.bfloat16), "fsdp", scatter_dimension=0, tiled=True
        ).astype(jnp.float32),
        lax.psum_scatter(
            grad_key.astype(jnp.bfloat16), "fsdp", scatter_dimension=0, tiled=True
        ).astype(jnp.float32),
        lax.psum_scatter(
            grad_value.astype(jnp.bfloat16), "fsdp", scatter_dimension=0, tiled=True
        ).astype(jnp.float32),
        lax.psum_scatter(
            grad_output.astype(jnp.bfloat16), "fsdp", scatter_dimension=0, tiled=True
        ).astype(jnp.float32),
        lax.psum_scatter(
            grad_gate.astype(jnp.bfloat16), "fsdp", scatter_dimension=0, tiled=True
        ).astype(jnp.float32),
        lax.psum_scatter(
            grad_up.astype(jnp.bfloat16), "fsdp", scatter_dimension=0, tiled=True
        ).astype(jnp.float32),
        lax.psum_scatter(
            grad_down.astype(jnp.bfloat16), "fsdp", scatter_dimension=0, tiled=True
        ).astype(jnp.float32),
        lax.psum_scatter(
            grad_attn.astype(jnp.bfloat16), "fsdp", scatter_dimension=0, tiled=True
        ).astype(jnp.float32),
        lax.psum_scatter(
            grad_ffn.astype(jnp.bfloat16), "fsdp", scatter_dimension=0, tiled=True
        ).astype(jnp.float32),
    )
    summed = (
        lax.psum(owned[0].astype(jnp.bfloat16), "ctx").astype(jnp.float32),
        lax.psum(owned[1].astype(jnp.bfloat16), "ctx").astype(jnp.float32),
        lax.psum(owned[2].astype(jnp.bfloat16), "ctx").astype(jnp.float32),
        lax.psum(owned[3].astype(jnp.bfloat16), "ctx").astype(jnp.float32),
        lax.psum(owned[4].astype(jnp.bfloat16), "ctx").astype(jnp.float32),
        lax.psum(owned[5].astype(jnp.bfloat16), "ctx").astype(jnp.float32),
        lax.psum(owned[6].astype(jnp.bfloat16), "ctx").astype(jnp.float32),
        lax.psum(owned[7].astype(jnp.bfloat16), "ctx").astype(jnp.float32),
        lax.psum(owned[8].astype(jnp.bfloat16), "ctx").astype(jnp.float32),
    )
    return (
        block_out,
        grad_tokens,
        summed[0],
        summed[1],
        summed[2],
        summed[3],
        summed[4],
        summed[5],
        summed[6],
        summed[7],
        summed[8],
    )


def solution(mesh):
    placed = (
        P("fsdp", "ctx", None),
        P("fsdp", "ctx"),
        P("fsdp", "ctx"),
        P("fsdp", None),
        P("fsdp", None),
        P("fsdp", None),
        P("fsdp", None),
        P("fsdp", None),
        P("fsdp", None),
        P("fsdp", None),
        P("fsdp"),
        P("fsdp"),
        P("fsdp", "ctx", None),
    )
    return jax.shard_map(
        local,
        mesh=mesh,
        in_specs=placed,
        out_specs=(
            P("fsdp", "ctx", None),
            P("fsdp", "ctx", None),
            P("fsdp", None),
            P("fsdp", None),
            P("fsdp", None),
            P("fsdp", None),
            P("fsdp", None),
            P("fsdp", None),
            P("fsdp", None),
            P("fsdp"),
            P("fsdp"),
        ),
        check_vma=False,
    )
```

```python
import functools
import math

import jax
import jax.numpy as jnp
from jax import lax
from jax.experimental import pallas as pl
from jax.experimental.pallas import tpu as pltpu
from jax.sharding import PartitionSpec as P

HEADS = 9
KV_HEADS = 3
HEAD_DIM = 64


epsilon = 1e-05
rope_base = 100000.0
masked_value = -1e30


def tables(places):
    half_dim = HEAD_DIM // 2
    frequency = rope_base ** (-(jnp.arange(half_dim, dtype=jnp.float32) * (2.0 / HEAD_DIM)))
    angles = frequency[:, None] * places.astype(jnp.float32)[None, :]
    return (jnp.cos(angles), jnp.sin(angles))


def rotate(values, cosine, sine, heads):
    half_dim = HEAD_DIM // 2
    halves = values.reshape(heads, 2, half_dim, -1)
    front = halves[:, 0]
    back = halves[:, 1]
    return jnp.stack(
        [front * cosine - back * sine, back * cosine + front * sine], axis=1
    ).reshape(heads * HEAD_DIM, -1)


def normalize_parts(values):
    inverse = lax.rsqrt(jnp.mean(values * values, axis=-1, keepdims=True) + epsilon)
    return (values * inverse, inverse)


def norm_back(grad_normed, scaled, inverse, gain_row):
    grad_scaled = grad_normed * gain_row
    return inverse * (grad_scaled - scaled * jnp.mean(grad_scaled * scaled, axis=-1, keepdims=True))


def forward_dot(left, right):
    return jnp.dot(left, right, preferred_element_type=jnp.float32)


def contract_rows(left, right):
    return lax.dot_general(
        left, right, (((0,), (0,)), ((), ())), preferred_element_type=jnp.float32
    )


def times_transposed(left, right):
    return lax.dot_general(
        left, right, (((1,), (1,)), ((), ())), preferred_element_type=jnp.float32
    )


def dot_tn(left, right):
    return lax.dot_general(
        left, right, (((0,), (0,)), ((), ())), preferred_element_type=jnp.float32
    )


def fill_bias(bias, row_ref, column_ref, block):
    length = bias.shape[0]
    for begin in range(0, length, block):
        end = begin + block
        keys = lax.broadcasted_iota(jnp.int32, (end, block), 0)
        places = lax.broadcasted_iota(jnp.int32, (end, block), 1) + begin
        same = column_ref[:end, :1] == row_ref[0, :, begin:end]
        bias[:end, begin:end] = jnp.where(same & (keys <= places), 0.0, masked_value)


def attend_kernel(block, q_ref, k_ref, v_ref, row_ref, column_ref, mixed_ref, total_ref, bias):
    @pl.when(pl.program_id(1) == 0)
    def _():
        fill_bias(bias, row_ref, column_ref, block)

    length = bias.shape[0]
    for begin in range(0, length, block):
        end = begin + block
        scores = dot_tn(k_ref[:, :end], q_ref[:, begin:end]) + bias[:end, begin:end]
        maxima = jnp.max(scores, axis=0, keepdims=True)
        exponent = jnp.exp(scores - maxima)
        totals = jnp.sum(exponent, axis=0, keepdims=True)
        mixed = jnp.dot(
            v_ref[:, :end], exponent.astype(jnp.bfloat16), preferred_element_type=jnp.float32
        )
        mixed_ref[:, begin:end] = (mixed / totals).astype(jnp.bfloat16)
        total_ref[0, 0, :, begin:end] = maxima + jnp.log(totals)


def rotate_back(values, cosine, sine):
    half_dim = HEAD_DIM // 2
    front = values[:half_dim]
    back = values[half_dim:]
    return jnp.concatenate([front * cosine + back * sine, back * cosine - front * sine], axis=0)


def attend_back_kernel(
    block,
    group,
    q_ref,
    k_ref,
    v_ref,
    grad_ref,
    mixed_ref,
    total_ref,
    row_ref,
    column_ref,
    cos_ref,
    sin_ref,
    dq_ref,
    dk_ref,
    dv_ref,
    bias,
    dk_sum,
    dv_sum,
):
    head = pl.program_id(1)

    @pl.when(head == 0)
    def _():
        fill_bias(bias, row_ref, column_ref, block)

    @pl.when(head % group == 0)
    def _():
        dk_sum[...] = jnp.zeros_like(dk_sum)
        dv_sum[...] = jnp.zeros_like(dv_sum)

    length = bias.shape[0]
    score_scale = 1.0 / math.sqrt(HEAD_DIM)
    for begin in range(0, length, block):
        end = begin + block
        query = q_ref[:, begin:end]
        grad = grad_ref[:, begin:end]
        centre = jnp.sum(
            grad.astype(jnp.float32) * mixed_ref[:, begin:end].astype(jnp.float32),
            axis=0,
            keepdims=True,
        )
        keys = k_ref[:, :end]
        scores = dot_tn(keys, query) + bias[:end, begin:end]
        probs = jnp.exp(scores - total_ref[0, 0, :, begin:end])
        grad_probs = dot_tn(v_ref[:, :end], grad)
        grad_scores = (probs * (grad_probs - centre)).astype(jnp.bfloat16)
        dv_sum[:, :end] += times_transposed(grad, probs.astype(jnp.bfloat16))
        dk_sum[:, :end] += times_transposed(query, grad_scores)
        dq = jnp.dot(keys, grad_scores, preferred_element_type=jnp.float32) * score_scale
        dq_ref[:, begin:end] = rotate_back(
            dq, cos_ref[:, begin:end], sin_ref[:, begin:end]
        ).astype(jnp.bfloat16)

    @pl.when(head % group == group - 1)
    def _():
        dk_ref[...] = rotate_back(dk_sum[...], cos_ref[...], sin_ref[...]).astype(jnp.bfloat16)
        dv_ref[...] = dv_sum[...].astype(jnp.bfloat16)


VMEM_LIMIT = 48 * 1024 * 1024


def specs(length, group):
    per_head = pl.BlockSpec((HEAD_DIM, length), lambda s, h: (h, s))
    per_key = pl.BlockSpec((HEAD_DIM, length), lambda s, h: (h // group, s))
    total = pl.BlockSpec((1, 1, 1, length), lambda s, h: (s, h, 0, 0))
    row = pl.BlockSpec((1, 1, length), lambda s, h: (s, 0, 0))
    column = pl.BlockSpec((length, 1), lambda s, h: (s, 0))
    table = pl.BlockSpec((HEAD_DIM // 2, length), lambda s, h: (0, s))
    return per_head, per_key, total, row, column, table


def attend(queries, keys, values, seg_row, seg_column, sequences, length):
    group = HEADS // KV_HEADS
    block = min(256, length)
    per_head, per_key, total, row, column, _ = specs(length, group)
    rows = sequences * length
    area = sequences * HEADS * length * (length + block) // 2
    return pl.pallas_call(
        functools.partial(attend_kernel, block),
        grid=(sequences, HEADS),
        in_specs=[per_head, per_key, per_key, row, column],
        out_specs=[per_head, total],
        out_shape=[
            jax.ShapeDtypeStruct((HEADS * HEAD_DIM, rows), jnp.bfloat16),
            jax.ShapeDtypeStruct((sequences, HEADS, 1, length), jnp.float32),
        ],
        scratch_shapes=[pltpu.VMEM((length, length), jnp.float32)],
        compiler_params=pltpu.CompilerParams(vmem_limit_bytes=VMEM_LIMIT),
        cost_estimate=pl.CostEstimate(
            flops=area * HEAD_DIM * 16, bytes_accessed=rows * 4096, transcendentals=area
        ),
        name="attend",
    )(queries, keys, values, seg_row, seg_column)


def attend_back(
    queries, keys, values, grads, mixed, totals, seg_row, seg_column, cosine, sine, sequences, length
):
    group = HEADS // KV_HEADS
    block = min(256, length)
    per_head, per_key, total, row, column, table = specs(length, group)
    rows = sequences * length
    area = sequences * HEADS * length * (length + block) // 2
    return pl.pallas_call(
        functools.partial(attend_back_kernel, block, group),
        grid=(sequences, HEADS),
        in_specs=[
            per_head,
            per_key,
            per_key,
            per_head,
            per_head,
            total,
            row,
            column,
            table,
            table,
        ],
        out_specs=[per_head, per_key, per_key],
        out_shape=[
            jax.ShapeDtypeStruct((HEADS * HEAD_DIM, rows), jnp.bfloat16),
            jax.ShapeDtypeStruct((KV_HEADS * HEAD_DIM, rows), jnp.bfloat16),
            jax.ShapeDtypeStruct((KV_HEADS * HEAD_DIM, rows), jnp.bfloat16),
        ],
        scratch_shapes=[
            pltpu.VMEM((length, length), jnp.float32),
            pltpu.VMEM((HEAD_DIM, length), jnp.float32),
            pltpu.VMEM((HEAD_DIM, length), jnp.float32),
        ],
        compiler_params=pltpu.CompilerParams(vmem_limit_bytes=VMEM_LIMIT),
        cost_estimate=pl.CostEstimate(
            flops=area * HEAD_DIM * 40, bytes_accessed=rows * 8192, transcendentals=area
        ),
        name="attend_back",
    )(queries, keys, values, grads, mixed, totals, seg_row, seg_column, cosine, sine)


MESH = pl.DeviceIdType.MESH


def pack_rows(rows):
    return -(-(rows + 2) // 16) * 16


def split_columns(parts, pieces):
    width = sum(part.shape[-1] for part in parts) // pieces
    out = []
    for piece in range(pieces):
        begin, end = piece * width, (piece + 1) * width
        taken, at = [], 0
        for part in parts:
            low, high = max(begin, at), min(end, at + part.shape[-1])
            if low < high:
                taken.append(part[..., low - at : high - at])
            at += part.shape[-1]
        out.append(jnp.concatenate(taken, axis=-1) if len(taken) > 1 else taken[0])
    return out


def join_columns(pieces, widths):
    width = pieces[0].shape[-1]
    out, at = [], 0
    for want in widths:
        taken = []
        for index, piece in enumerate(pieces):
            low, high = max(at, index * width), min(at + want, (index + 1) * width)
            if low < high:
                taken.append(piece[..., low - index * width : high - index * width])
        out.append(jnp.concatenate(taken, axis=-1) if len(taken) > 1 else taken[0])
        at += want
    return out


def greet(shards, parts, me, mine):
    barrier = pltpu.get_barrier_semaphore()

    def shard(step, carry):
        pl.semaphore_signal(
            barrier, inc=1, device_id=(lax.rem(me + step, shards), mine), device_id_type=MESH
        )
        return carry

    def part(step, carry):
        pl.semaphore_signal(
            barrier, inc=1, device_id=(me, lax.rem(mine + step, parts)), device_id_type=MESH
        )
        return carry

    lax.fori_loop(1, shards, shard, 0)
    lax.fori_loop(1, parts, part, 0)
    pl.semaphore_wait(barrier, shards + parts - 2)


def exchange(source, target, width, length, parts, me, mine, send, recv, inward):
    def at_source(index):
        if inward:
            return source.at[pl.ds(index * width, width)]
        return source.at[:, pl.ds(index * length, length)]

    def at_target(index):
        if inward:
            return target.at[:, pl.ds(index * length, length)]
        return target.at[pl.ds(index * width, width)]

    def copy(step):
        other = lax.rem(mine + step, parts)
        return pltpu.make_async_remote_copy(
            src_ref=at_source(other),
            dst_ref=at_target(mine),
            send_sem=send.at[other],
            recv_sem=recv.at[mine],
            device_id=(me, other),
            device_id_type=MESH,
        )

    def arrival(step):
        other = lax.rem(mine + step, parts)
        return pltpu.make_async_remote_copy(
            src_ref=at_source(other),
            dst_ref=at_target(other),
            send_sem=send.at[other],
            recv_sem=recv.at[other],
            device_id=(me, other),
            device_id_type=MESH,
        )

    own = pltpu.make_async_copy(at_source(mine), at_target(mine), recv.at[mine])

    def start():
        for step in range(1, parts):
            copy(step).start()
        own.start()

    def finish():
        own.wait()
        for step in range(1, parts):
            arrival(step).wait_recv()
            copy(step).wait_send()

    return start, finish


def enter_kernel(
    shards,
    parts,
    width,
    length,
    tokens,
    cotangent,
    places,
    weights,
    tokens_out,
    cotangent_out,
    places_out,
    weights_out,
    exchange_send,
    exchange_recv,
    first_send,
    second_send,
    third_send,
    weight_recv,
    own_sem,
):
    me, mine = lax.axis_index("fsdp"), lax.axis_index("ctx")
    chips = parts // 2
    core = lax.rem(mine, 2)
    chip = mine // 2
    twin = chip * 2 + 1 - core
    greet(shards, parts, me, mine)
    moves = []
    for index, (source, target) in enumerate(
        ((tokens, tokens_out), (places, places_out), (cotangent, cotangent_out))
    ):
        step_width, step_length = (1, 1) if index == 1 else (width, length)
        moves.append(
            exchange(
                source,
                target,
                step_width,
                step_length,
                parts,
                me,
                mine,
                exchange_send.at[index],
                exchange_recv.at[index],
                True,
            )
        )
    own = pltpu.make_async_copy(weights, weights_out.at[me], own_sem)
    own.start()

    def piece(source, index, send, device):
        return pltpu.make_async_remote_copy(
            src_ref=weights_out.at[source, index],
            dst_ref=weights_out.at[source, index],
            send_sem=send,
            recv_sem=weight_recv.at[source, index],
            device_id=device,
            device_id_type=MESH,
        )

    def first(step):
        other = lax.rem(me + step, shards)
        return pltpu.make_async_remote_copy(
            src_ref=weights.at[mine],
            dst_ref=weights_out.at[me, mine],
            send_sem=first_send.at[other],
            recv_sem=weight_recv.at[me, mine],
            device_id=(other, mine),
            device_id_type=MESH,
        )

    def second(source, hop):
        other = lax.rem(chip + hop, chips) * 2 + core
        return piece(source, mine, second_send.at[source, hop], (me, other))

    def third(source, hop):
        index = lax.rem(chip + hop, chips) * 2 + core
        return piece(source, index, third_send.at[source, hop], (me, twin))

    def arrived(source, index):
        piece(source, index, third_send.at[source, 0], (me, twin)).wait_recv()

    def loop(body):
        def run(step, carry):
            body(step)
            return carry

        lax.fori_loop(1, shards, run, 0)

    loop(lambda step: first(step).start())
    moves[0][0]()
    moves[1][0]()

    def spread(step):
        source = lax.rem(me + shards - step, shards)
        arrived(source, mine)
        for hop in range(1, chips):
            second(source, hop).start()
        third(source, 0).start()

    loop(spread)
    moves[2][0]()

    def relay(step):
        source = lax.rem(me + shards - step, shards)
        for hop in range(1, chips):
            arrived(source, lax.rem(chip + hop, chips) * 2 + core)
            third(source, hop).start()

    loop(relay)

    def collect(step):
        source = lax.rem(me + shards - step, shards)
        for hop in range(chips):
            arrived(source, lax.rem(chip + hop, chips) * 2 + 1 - core)

    loop(collect)

    def drain(step):
        source = lax.rem(me + shards - step, shards)
        first(step).wait_send()
        for hop in range(1, chips):
            second(source, hop).wait_send()
        for hop in range(chips):
            third(source, hop).wait_send()

    loop(drain)
    own.wait()
    for _, finish in moves:
        finish()


def enter_call(shards, parts, tokens, cotangent, places, weights):
    count, length, model_width = tokens.shape
    width = count // parts
    whole = jax.ShapeDtypeStruct((width, length * parts, model_width), tokens.dtype)
    dma = pltpu.SemaphoreType.DMA
    return pl.pallas_call(
        functools.partial(enter_kernel, shards, parts, width, length),
        out_shape=[
            whole,
            whole,
            jax.ShapeDtypeStruct((1, parts) + places.shape[2:], places.dtype),
            jax.ShapeDtypeStruct((shards,) + weights.shape, weights.dtype),
        ],
        in_specs=[pl.BlockSpec(memory_space=pl.ANY)] * 4,
        out_specs=[pl.BlockSpec(memory_space=pl.ANY)] * 4,
        scratch_shapes=[
            dma((3, parts)),
            dma((3, parts)),
            dma((shards,)),
            dma((shards, parts)),
            dma((shards, parts)),
            dma((shards, parts)),
            dma,
        ],
        compiler_params=pltpu.CompilerParams(collective_id=0, has_side_effects=True),
        name="enter",
    )(tokens, cotangent, places, weights)


def leave_kernel(
    shards,
    parts,
    width,
    length,
    block_in,
    tokens_in,
    grads,
    block_out,
    tokens_out,
    summed,
    twin_in,
    chip_send,
    chip_in,
    shard_send,
    shard_in,
    result,
    exchange_send,
    exchange_recv,
    twin_sends,
    twin_recvs,
    chip_sends,
    chip_recvs,
    shard_sends,
    shard_recvs,
    last_sends,
    last_recvs,
):
    me, mine = lax.axis_index("fsdp"), lax.axis_index("ctx")
    chips = parts // 2
    core = lax.rem(mine, 2)
    chip = mine // 2
    twin = chip * 2 + 1 - core
    greet(shards, parts, me, mine)
    moves = [
        exchange(
            source,
            target,
            width,
            length,
            parts,
            me,
            mine,
            exchange_send.at[index],
            exchange_recv.at[index],
            False,
        )
        for index, (source, target) in enumerate(((block_in, block_out), (tokens_in, tokens_out)))
    ]

    def loop(body):
        def run(step, carry):
            body(step)
            return carry

        lax.fori_loop(1, shards + 1, run, 0)

    def to_twin(target, hop):
        index = lax.rem(chip + hop, chips)
        return pltpu.make_async_remote_copy(
            src_ref=grads.at[target, index * 2 + 1 - core],
            dst_ref=twin_in.at[target, index],
            send_sem=twin_sends.at[target, index],
            recv_sem=twin_recvs.at[target, index],
            device_id=(me, twin),
            device_id_type=MESH,
        )

    def to_chip(target, hop):
        other = lax.rem(chip + hop, chips)
        return pltpu.make_async_remote_copy(
            src_ref=chip_send.at[target, other],
            dst_ref=chip_in.at[target, chip],
            send_sem=chip_sends.at[target, other],
            recv_sem=chip_recvs.at[target, chip],
            device_id=(me, other * 2 + core),
            device_id_type=MESH,
        )

    def from_chip(target, hop):
        other = lax.rem(chip + hop, chips)
        return pltpu.make_async_remote_copy(
            src_ref=chip_send.at[target, other],
            dst_ref=chip_in.at[target, other],
            send_sem=chip_sends.at[target, other],
            recv_sem=chip_recvs.at[target, other],
            device_id=(me, other * 2 + core),
            device_id_type=MESH,
        )

    def to_shard(target):
        return pltpu.make_async_remote_copy(
            src_ref=shard_send.at[target],
            dst_ref=shard_in.at[me],
            send_sem=shard_sends.at[target],
            recv_sem=shard_recvs.at[me],
            device_id=(target, mine),
            device_id_type=MESH,
        )

    def from_shard(source):
        return pltpu.make_async_remote_copy(
            src_ref=shard_send.at[source],
            dst_ref=shard_in.at[source],
            send_sem=shard_sends.at[source],
            recv_sem=shard_recvs.at[source],
            device_id=(source, mine),
            device_id_type=MESH,
        )

    def to_part(step):
        other = lax.rem(mine + step, parts)
        return pltpu.make_async_remote_copy(
            src_ref=result,
            dst_ref=summed.at[mine],
            send_sem=last_sends.at[other],
            recv_sem=last_recvs.at[mine],
            device_id=(me, other),
            device_id_type=MESH,
        )

    def from_part(step):
        other = lax.rem(mine + step, parts)
        return pltpu.make_async_remote_copy(
            src_ref=result,
            dst_ref=summed.at[other],
            send_sem=last_sends.at[other],
            recv_sem=last_recvs.at[other],
            device_id=(me, other),
            device_id_type=MESH,
        )

    def send_twin(step):
        for hop in range(1, chips + 1):
            to_twin(lax.rem(me + step, shards), hop).start()

    loop(send_twin)

    def wide(values):
        return values.astype(jnp.float32)

    def send_chip(step):
        target = lax.rem(me + step, shards)
        for hop in range(1, chips):
            other = lax.rem(chip + hop, chips)
            to_twin(target, hop).wait_recv()
            chip_send[target, other] = (
                wide(grads[target, other * 2 + core]) + wide(twin_in[target, other])
            ).astype(jnp.bfloat16)
            to_chip(target, hop).start()
        to_twin(target, chips).wait_recv()

    loop(send_chip)
    for start, _ in moves:
        start()

    def whole_sum(target):
        total = wide(grads[target, mine]) + wide(twin_in[target, chip])
        for hop in range(1, chips):
            from_chip(target, hop).wait_recv()
            total = total + wide(chip_in[target, lax.rem(chip + hop, chips)])
        return total

    def send_shard(step, carry):
        target = lax.rem(me + step, shards)
        shard_send[target] = whole_sum(target).astype(jnp.bfloat16)
        to_shard(target).start()
        return carry

    lax.fori_loop(1, shards, send_shard, 0)
    shard_send[me] = whole_sum(me).astype(jnp.bfloat16)

    def add_shard(step, total):
        source = lax.rem(me + shards - step, shards)
        from_shard(source).wait_recv()
        return total + wide(shard_in[source])

    result[...] = lax.fori_loop(1, shards, add_shard, wide(shard_send[me])).astype(jnp.bfloat16)
    own = pltpu.make_async_copy(result, summed.at[mine], last_recvs.at[mine])
    own.start()
    for step in range(1, parts):
        to_part(step).start()
    own.wait()
    for step in range(1, parts):
        from_part(step).wait_recv()
        to_part(step).wait_send()

    def drain(step):
        target = lax.rem(me + step, shards)
        for hop in range(1, chips + 1):
            to_twin(target, hop).wait_send()
        for hop in range(1, chips):
            to_chip(target, hop).wait_send()

    loop(drain)

    def drain_shard(step, carry):
        to_shard(lax.rem(me + step, shards)).wait_send()
        return carry

    lax.fori_loop(1, shards, drain_shard, 0)
    for _, finish in moves:
        finish()


def leave_call(shards, parts, block_out, grad_tokens, grads):
    width, full_len, model_width = block_out.shape
    length = full_len // parts
    tile = grads.shape[2:]
    part = jax.ShapeDtypeStruct((width * parts, length, model_width), block_out.dtype)
    dma = pltpu.SemaphoreType.DMA
    chips = parts // 2
    any_space = pl.BlockSpec(memory_space=pl.ANY)
    on_chip = pl.BlockSpec(memory_space=pltpu.VMEM)
    return pl.pallas_call(
        functools.partial(leave_kernel, shards, parts, width, length),
        out_shape=[part, part, jax.ShapeDtypeStruct((parts,) + tile, jnp.bfloat16)],
        in_specs=[any_space, any_space, on_chip],
        out_specs=[any_space, any_space, on_chip],
        scratch_shapes=[
            pltpu.VMEM((shards, chips) + tile, jnp.bfloat16),
            pltpu.VMEM((shards, chips) + tile, jnp.bfloat16),
            pltpu.VMEM((shards, chips) + tile, jnp.bfloat16),
            pltpu.VMEM((shards,) + tile, jnp.bfloat16),
            pltpu.VMEM((shards,) + tile, jnp.bfloat16),
            pltpu.VMEM(tile, jnp.bfloat16),
            dma((2, parts)),
            dma((2, parts)),
            dma((shards, chips)),
            dma((shards, chips)),
            dma((shards, chips)),
            dma((shards, chips)),
            dma((shards,)),
            dma((shards,)),
            dma((parts,)),
            dma((parts,)),
        ],
        compiler_params=pltpu.CompilerParams(
            collective_id=1, has_side_effects=True, vmem_limit_bytes=VMEM_LIMIT
        ),
        name="leave",
    )(block_out, grad_tokens, grads)


def local(
    tokens,
    segments,
    positions,
    query_weight,
    key_weight,
    value_weight,
    output_weight,
    gate_weight,
    up_weight,
    down_weight,
    attn_gain,
    ffn_gain,
    cotangent,
):
    shards, parts = lax.axis_size("fsdp"), lax.axis_size("ctx")
    own_rows = query_weight.shape[0]
    packed_rows = pack_rows(own_rows)
    wide = (
        query_weight,
        key_weight,
        value_weight,
        output_weight,
        gate_weight,
        up_weight,
        down_weight.reshape(own_rows, -1),
    )
    widths = [part.shape[1] for part in wide]
    pieces = split_columns(wide, parts)
    columns = pieces[0].shape[1]

    def with_gains(pieces, attn_row, ffn_row):
        lead = attn_row.shape[:-1]
        room = [(0, 0)] * len(lead)
        gains = jnp.stack([attn_row, ffn_row], axis=-2)
        gains = jnp.pad(
            gains, room + [(0, packed_rows - own_rows - 2), (0, columns - own_rows)]
        )
        return jnp.stack(
            [
                jnp.concatenate([piece, gains if index == 0 else jnp.zeros_like(gains)], axis=-2)
                for index, piece in enumerate(pieces)
            ],
            axis=-3,
        )

    count, local_len, _ = tokens.shape
    per_part = count // parts
    places = jnp.concatenate(
        [
            segments.reshape(parts, per_part, local_len),
            positions.reshape(parts, per_part, local_len),
        ],
        axis=1,
    )
    place_rows = -(-2 * per_part // 8) * 8
    places = jnp.pad(places, ((0, 0), (0, place_rows - 2 * per_part), (0, 0)))
    tokens, cotangent, places, gathered = enter_call(
        shards,
        parts,
        tokens,
        cotangent,
        places[:, None],
        with_gains(pieces, attn_gain, ffn_gain),
    )
    places = jnp.transpose(places[0], (1, 0, 2)).reshape(place_rows, -1)
    segments = places[:per_part]
    positions = places[per_part : 2 * per_part]
    full = join_columns([gathered[:, index, :own_rows] for index in range(parts)], widths)
    full_query, full_key, full_value, full_output, full_gate, full_up = (
        part.reshape(shards * own_rows, -1) for part in full[:6]
    )
    full_down = full[6].reshape(-1, tokens.shape[2])
    full_attn = gathered[:, 0, own_rows, :own_rows].reshape(-1)
    full_ffn = gathered[:, 0, own_rows + 1, :own_rows].reshape(-1)
    seq_count, full_len, model_width = tokens.shape
    row_count = seq_count * full_len
    score_scale = 1.0 / math.sqrt(HEAD_DIM)
    attn_scale = full_attn.astype(jnp.float32)
    ffn_scale = full_ffn.astype(jnp.float32)
    inputs = tokens.astype(jnp.float32).reshape(row_count, model_width)
    scaled_one, inverse_one = normalize_parts(inputs)
    normed_one = (scaled_one * attn_scale).astype(jnp.bfloat16)
    def features(weight, rows):
        return lax.dot_general(
            weight, rows, (((0,), (1,)), ((), ())), preferred_element_type=jnp.float32
        )

    cosine, sine = tables(positions.reshape(row_count))
    queries = (rotate(features(full_query, normed_one), cosine, sine, HEADS) * score_scale).astype(
        jnp.bfloat16
    )
    key_rows = rotate(features(full_key, normed_one), cosine, sine, KV_HEADS).astype(jnp.bfloat16)
    value_rows = features(full_value, normed_one).astype(jnp.bfloat16)
    seg_row = segments.reshape(seq_count, 1, full_len)
    seg_column = segments.reshape(row_count, 1)
    mixed_rows, log_totals = attend(
        queries, key_rows, value_rows, seg_row, seg_column, seq_count, full_len
    )
    middle = inputs + dot_tn(mixed_rows, full_output)
    scaled_two, inverse_two = normalize_parts(middle)
    normed_two = (scaled_two * ffn_scale).astype(jnp.bfloat16)
    gate_pre = forward_dot(normed_two, full_gate)
    up_pre = forward_dot(normed_two, full_up)
    sigmoid_gate = jax.nn.sigmoid(gate_pre)
    silu_gate = gate_pre * sigmoid_gate
    hidden = (silu_gate * up_pre).astype(jnp.bfloat16)
    block_out = (middle + forward_dot(hidden, full_down)).astype(jnp.bfloat16).reshape(tokens.shape)
    grad_rows = cotangent.astype(jnp.float32).reshape(row_count, model_width)
    grad_low = grad_rows.astype(jnp.bfloat16)
    grad_down = contract_rows(hidden, grad_low)
    grad_hidden = times_transposed(grad_low, full_down)
    grad_up_in = (grad_hidden * silu_gate).astype(jnp.bfloat16)
    grad_gate_in = (
        grad_hidden * up_pre * sigmoid_gate * (1.0 + gate_pre * (1.0 - sigmoid_gate))
    ).astype(jnp.bfloat16)
    grad_gate = contract_rows(normed_two, grad_gate_in)
    grad_up = contract_rows(normed_two, grad_up_in)
    grad_normed_two = times_transposed(grad_gate_in, full_gate) + times_transposed(
        grad_up_in, full_up
    )
    grad_ffn = jnp.sum(grad_normed_two * scaled_two, axis=0)
    grad_middle = grad_rows + norm_back(grad_normed_two, scaled_two, inverse_two, ffn_scale)
    grad_branch = grad_middle.astype(jnp.bfloat16)
    grad_output = forward_dot(mixed_rows, grad_branch)
    grad_mixed = times_transposed(full_output, grad_branch).astype(jnp.bfloat16)
    grad_query_in, grad_key_in, grad_value_in = attend_back(
        queries,
        key_rows,
        value_rows,
        grad_mixed,
        mixed_rows,
        log_totals,
        seg_row,
        seg_column,
        cosine,
        sine,
        seq_count,
        full_len,
    )

    def weight_grad(grads):
        return lax.dot_general(
            normed_one, grads, (((0,), (1,)), ((), ())), preferred_element_type=jnp.float32
        )

    def row_grad(grads, weight):
        return lax.dot_general(
            grads, weight, (((0,), (1,)), ((), ())), preferred_element_type=jnp.float32
        )

    grad_query = weight_grad(grad_query_in)
    grad_key = weight_grad(grad_key_in)
    grad_value = weight_grad(grad_value_in)
    grad_normed_one = (
        row_grad(grad_query_in, full_query)
        + row_grad(grad_key_in, full_key)
        + row_grad(grad_value_in, full_value)
    )
    grad_attn = jnp.sum(grad_normed_one * scaled_one, axis=0)
    grad_tokens = (
        (grad_middle + norm_back(grad_normed_one, scaled_one, inverse_one, attn_scale))
        .astype(jnp.bfloat16)
        .reshape(tokens.shape)
    )
    grads = [
        grad.astype(jnp.bfloat16).reshape(shards, own_rows, -1)
        for grad in (
            grad_query,
            grad_key,
            grad_value,
            grad_output,
            grad_gate,
            grad_up,
            grad_down.astype(jnp.bfloat16),
        )
    ]
    packed = with_gains(
        split_columns(grads, parts),
        grad_attn.astype(jnp.bfloat16).reshape(shards, own_rows),
        grad_ffn.astype(jnp.bfloat16).reshape(shards, own_rows),
    )
    block_out, grad_tokens, summed = leave_call(shards, parts, block_out, grad_tokens, packed)
    summed = summed.astype(jnp.float32)
    owned = join_columns([summed[index, :own_rows] for index in range(parts)], widths)
    owned[6] = owned[6].reshape(down_weight.shape)
    return (
        block_out,
        grad_tokens,
        *owned,
        summed[0, own_rows, :own_rows],
        summed[0, own_rows + 1, :own_rows],
    )


def solution(mesh):
    placed = (
        P("fsdp", "ctx", None),
        P("fsdp", "ctx"),
        P("fsdp", "ctx"),
        P("fsdp", None),
        P("fsdp", None),
        P("fsdp", None),
        P("fsdp", None),
        P("fsdp", None),
        P("fsdp", None),
        P("fsdp", None),
        P("fsdp"),
        P("fsdp"),
        P("fsdp", "ctx", None),
    )
    return jax.shard_map(
        local,
        mesh=mesh,
        in_specs=placed,
        out_specs=(
            P("fsdp", "ctx", None),
            P("fsdp", "ctx", None),
            P("fsdp", None),
            P("fsdp", None),
            P("fsdp", None),
            P("fsdp", None),
            P("fsdp", None),
            P("fsdp", None),
            P("fsdp", None),
            P("fsdp"),
            P("fsdp"),
        ),
        check_vma=False,
    )
```

```python
import functools
import math

import jax
import jax.numpy as jnp
from jax import lax
from jax.experimental import pallas as pl
from jax.experimental.pallas import tpu as pltpu
from jax.sharding import PartitionSpec as P

HEADS = 9
KV_HEADS = 3
HEAD_DIM = 64


epsilon = 1e-05
rope_base = 100000.0
masked_value = -1e30


def tables(places):
    half_dim = HEAD_DIM // 2
    frequency = rope_base ** (-(jnp.arange(half_dim, dtype=jnp.float32) * (2.0 / HEAD_DIM)))
    angles = frequency[:, None] * places.astype(jnp.float32)[None, :]
    return (jnp.cos(angles), jnp.sin(angles))


def rotate(values, cosine, sine, heads):
    half_dim = HEAD_DIM // 2
    halves = values.reshape(heads, 2, half_dim, -1)
    front = halves[:, 0]
    back = halves[:, 1]
    return jnp.stack(
        [front * cosine - back * sine, back * cosine + front * sine], axis=1
    ).reshape(heads * HEAD_DIM, -1)


def normalize_parts(values):
    inverse = lax.rsqrt(jnp.mean(values * values, axis=-1, keepdims=True) + epsilon)
    return (values * inverse, inverse)


def norm_back(grad_normed, scaled, inverse, gain_row):
    grad_scaled = grad_normed * gain_row
    return inverse * (grad_scaled - scaled * jnp.mean(grad_scaled * scaled, axis=-1, keepdims=True))


def forward_dot(left, right):
    return jnp.dot(left, right, preferred_element_type=jnp.float32)


def contract_rows(left, right):
    return lax.dot_general(
        left, right, (((0,), (0,)), ((), ())), preferred_element_type=jnp.float32
    )


def times_transposed(left, right):
    return lax.dot_general(
        left, right, (((1,), (1,)), ((), ())), preferred_element_type=jnp.float32
    )


def dot_tn(left, right):
    return lax.dot_general(
        left, right, (((0,), (0,)), ((), ())), preferred_element_type=jnp.float32
    )


def fill_bias(bias, row_ref, column_ref, block):
    length = bias.shape[0]
    for begin in range(0, length, block):
        end = begin + block
        keys = lax.broadcasted_iota(jnp.int32, (end, block), 0)
        places = lax.broadcasted_iota(jnp.int32, (end, block), 1) + begin
        same = column_ref[:end, :1] == row_ref[0, :, begin:end]
        bias[:end, begin:end] = jnp.where(same & (keys <= places), 0.0, masked_value)


def attend_kernel(block, q_ref, k_ref, v_ref, row_ref, column_ref, mixed_ref, total_ref, bias):
    @pl.when(pl.program_id(1) == 0)
    def _():
        fill_bias(bias, row_ref, column_ref, block)

    length = bias.shape[0]
    for begin in range(0, length, block):
        end = begin + block
        scores = dot_tn(k_ref[:, :end], q_ref[:, begin:end]) + bias[:end, begin:end]
        maxima = jnp.max(scores, axis=0, keepdims=True)
        exponent = jnp.exp(scores - maxima)
        totals = jnp.sum(exponent, axis=0, keepdims=True)
        mixed = jnp.dot(
            v_ref[:, :end], exponent.astype(jnp.bfloat16), preferred_element_type=jnp.float32
        )
        mixed_ref[:, begin:end] = (mixed / totals).astype(jnp.bfloat16)
        total_ref[0, 0, :, begin:end] = maxima + jnp.log(totals)


def rotate_back(values, cosine, sine):
    half_dim = HEAD_DIM // 2
    front = values[:half_dim]
    back = values[half_dim:]
    return jnp.concatenate([front * cosine + back * sine, back * cosine - front * sine], axis=0)


def attend_back_kernel(
    block,
    group,
    q_ref,
    k_ref,
    v_ref,
    grad_ref,
    mixed_ref,
    total_ref,
    row_ref,
    column_ref,
    cos_ref,
    sin_ref,
    dq_ref,
    dk_ref,
    dv_ref,
    bias,
    dk_sum,
    dv_sum,
):
    head = pl.program_id(1)

    @pl.when(head == 0)
    def _():
        fill_bias(bias, row_ref, column_ref, block)

    @pl.when(head % group == 0)
    def _():
        dk_sum[...] = jnp.zeros_like(dk_sum)
        dv_sum[...] = jnp.zeros_like(dv_sum)

    length = bias.shape[0]
    score_scale = 1.0 / math.sqrt(HEAD_DIM)
    for begin in range(0, length, block):
        end = begin + block
        query = q_ref[:, begin:end]
        grad = grad_ref[:, begin:end]
        centre = jnp.sum(
            grad.astype(jnp.float32) * mixed_ref[:, begin:end].astype(jnp.float32),
            axis=0,
            keepdims=True,
        )
        keys = k_ref[:, :end]
        scores = dot_tn(keys, query) + bias[:end, begin:end]
        probs = jnp.exp(scores - total_ref[0, 0, :, begin:end])
        grad_probs = dot_tn(v_ref[:, :end], grad)
        grad_scores = (probs * (grad_probs - centre)).astype(jnp.bfloat16)
        dv_sum[:, :end] += times_transposed(grad, probs.astype(jnp.bfloat16))
        dk_sum[:, :end] += times_transposed(query, grad_scores)
        dq = jnp.dot(keys, grad_scores, preferred_element_type=jnp.float32) * score_scale
        dq_ref[:, begin:end] = rotate_back(
            dq, cos_ref[:, begin:end], sin_ref[:, begin:end]
        ).astype(jnp.bfloat16)

    @pl.when(head % group == group - 1)
    def _():
        dk_ref[...] = rotate_back(dk_sum[...], cos_ref[...], sin_ref[...]).astype(jnp.bfloat16)
        dv_ref[...] = dv_sum[...].astype(jnp.bfloat16)


VMEM_LIMIT = 48 * 1024 * 1024


def specs(length, group):
    per_head = pl.BlockSpec((HEAD_DIM, length), lambda s, h: (h, s))
    per_key = pl.BlockSpec((HEAD_DIM, length), lambda s, h: (h // group, s))
    total = pl.BlockSpec((1, 1, 1, length), lambda s, h: (s, h, 0, 0))
    row = pl.BlockSpec((1, 1, length), lambda s, h: (s, 0, 0))
    column = pl.BlockSpec((length, 1), lambda s, h: (s, 0))
    table = pl.BlockSpec((HEAD_DIM // 2, length), lambda s, h: (0, s))
    return per_head, per_key, total, row, column, table


def attend(queries, keys, values, seg_row, seg_column, sequences, length):
    group = HEADS // KV_HEADS
    block = min(256, length)
    per_head, per_key, total, row, column, _ = specs(length, group)
    rows = sequences * length
    area = sequences * HEADS * length * (length + block) // 2
    return pl.pallas_call(
        functools.partial(attend_kernel, block),
        grid=(sequences, HEADS),
        in_specs=[per_head, per_key, per_key, row, column],
        out_specs=[per_head, total],
        out_shape=[
            jax.ShapeDtypeStruct((HEADS * HEAD_DIM, rows), jnp.bfloat16),
            jax.ShapeDtypeStruct((sequences, HEADS, 1, length), jnp.float32),
        ],
        scratch_shapes=[pltpu.VMEM((length, length), jnp.float32)],
        compiler_params=pltpu.CompilerParams(vmem_limit_bytes=VMEM_LIMIT),
        cost_estimate=pl.CostEstimate(
            flops=area * HEAD_DIM * 16, bytes_accessed=rows * 4096, transcendentals=area
        ),
        name="attend",
    )(queries, keys, values, seg_row, seg_column)


def attend_back(
    queries, keys, values, grads, mixed, totals, seg_row, seg_column, cosine, sine, sequences, length
):
    group = HEADS // KV_HEADS
    block = min(256, length)
    per_head, per_key, total, row, column, table = specs(length, group)
    rows = sequences * length
    area = sequences * HEADS * length * (length + block) // 2
    return pl.pallas_call(
        functools.partial(attend_back_kernel, block, group),
        grid=(sequences, HEADS),
        in_specs=[
            per_head,
            per_key,
            per_key,
            per_head,
            per_head,
            total,
            row,
            column,
            table,
            table,
        ],
        out_specs=[per_head, per_key, per_key],
        out_shape=[
            jax.ShapeDtypeStruct((HEADS * HEAD_DIM, rows), jnp.bfloat16),
            jax.ShapeDtypeStruct((KV_HEADS * HEAD_DIM, rows), jnp.bfloat16),
            jax.ShapeDtypeStruct((KV_HEADS * HEAD_DIM, rows), jnp.bfloat16),
        ],
        scratch_shapes=[
            pltpu.VMEM((length, length), jnp.float32),
            pltpu.VMEM((HEAD_DIM, length), jnp.float32),
            pltpu.VMEM((HEAD_DIM, length), jnp.float32),
        ],
        compiler_params=pltpu.CompilerParams(vmem_limit_bytes=VMEM_LIMIT),
        cost_estimate=pl.CostEstimate(
            flops=area * HEAD_DIM * 40, bytes_accessed=rows * 8192, transcendentals=area
        ),
        name="attend_back",
    )(queries, keys, values, grads, mixed, totals, seg_row, seg_column, cosine, sine)


MESH = pl.DeviceIdType.MESH


def pack_rows(rows):
    return -(-(rows + 2) // 16) * 16


def split_columns(parts, pieces):
    width = sum(part.shape[-1] for part in parts) // pieces
    out = []
    for piece in range(pieces):
        begin, end = piece * width, (piece + 1) * width
        taken, at = [], 0
        for part in parts:
            low, high = max(begin, at), min(end, at + part.shape[-1])
            if low < high:
                taken.append(part[..., low - at : high - at])
            at += part.shape[-1]
        out.append(jnp.concatenate(taken, axis=-1) if len(taken) > 1 else taken[0])
    return out


def join_columns(pieces, widths):
    width = pieces[0].shape[-1]
    out, at = [], 0
    for want in widths:
        taken = []
        for index, piece in enumerate(pieces):
            low, high = max(at, index * width), min(at + want, (index + 1) * width)
            if low < high:
                taken.append(piece[..., low - index * width : high - index * width])
        out.append(jnp.concatenate(taken, axis=-1) if len(taken) > 1 else taken[0])
        at += want
    return out


def greet(shards, parts, me, mine):
    barrier = pltpu.get_barrier_semaphore()

    def shard(step, carry):
        pl.semaphore_signal(
            barrier, inc=1, device_id=(lax.rem(me + step, shards), mine), device_id_type=MESH
        )
        return carry

    def part(step, carry):
        pl.semaphore_signal(
            barrier, inc=1, device_id=(me, lax.rem(mine + step, parts)), device_id_type=MESH
        )
        return carry

    lax.fori_loop(1, shards, shard, 0)
    lax.fori_loop(1, parts, part, 0)
    pl.semaphore_wait(barrier, shards + parts - 2)


def exchange(source, target, width, length, parts, me, mine, send, recv, inward):
    def at_source(index):
        if inward:
            return source.at[pl.ds(index * width, width)]
        return source.at[:, pl.ds(index * length, length)]

    def at_target(index):
        if inward:
            return target.at[:, pl.ds(index * length, length)]
        return target.at[pl.ds(index * width, width)]

    def copy(step):
        other = lax.rem(mine + step, parts)
        return pltpu.make_async_remote_copy(
            src_ref=at_source(other),
            dst_ref=at_target(mine),
            send_sem=send.at[other],
            recv_sem=recv.at[mine],
            device_id=(me, other),
            device_id_type=MESH,
        )

    def arrival(step):
        other = lax.rem(mine + step, parts)
        return pltpu.make_async_remote_copy(
            src_ref=at_source(other),
            dst_ref=at_target(other),
            send_sem=send.at[other],
            recv_sem=recv.at[other],
            device_id=(me, other),
            device_id_type=MESH,
        )

    own = pltpu.make_async_copy(at_source(mine), at_target(mine), recv.at[mine])

    def start():
        for step in range(1, parts):
            copy(step).start()
        own.start()

    def finish():
        own.wait()
        for step in range(1, parts):
            arrival(step).wait_recv()
            copy(step).wait_send()

    return start, finish


def enter_kernel(
    shards,
    parts,
    width,
    length,
    tokens,
    cotangent,
    places,
    weights,
    tokens_out,
    cotangent_out,
    places_out,
    weights_out,
    exchange_send,
    exchange_recv,
    first_send,
    second_send,
    third_send,
    weight_recv,
    own_sem,
):
    me, mine = lax.axis_index("fsdp"), lax.axis_index("ctx")
    across = parts // 2
    rows = shards // across
    row, column = me // across, lax.rem(me, across)
    core = lax.rem(mine, 2)
    chip = mine // 2
    twin = chip * 2 + 1 - core
    greet(shards, parts, me, mine)
    moves = []
    for index, (source, target) in enumerate(
        ((tokens, tokens_out), (places, places_out), (cotangent, cotangent_out))
    ):
        step_width, step_length = (1, 1) if index == 1 else (width, length)
        moves.append(
            exchange(
                source,
                target,
                step_width,
                step_length,
                parts,
                me,
                mine,
                exchange_send.at[index],
                exchange_recv.at[index],
                True,
            )
        )
    own = pltpu.make_async_copy(weights, weights_out.at[me], own_sem)
    own.start()

    def copy(source, index, origin, send, device):
        return pltpu.make_async_remote_copy(
            src_ref=origin,
            dst_ref=weights_out.at[source, index],
            send_sem=send,
            recv_sem=weight_recv.at[source, index],
            device_id=device,
            device_id_type=MESH,
        )

    def first(step):
        other = lax.rem(row + step, rows) * across + column
        return copy(me, core, weights.at[core], first_send.at[step], (other, mine))

    def second(source, hop, origin):
        other = row * across + lax.rem(column + hop, across)
        return copy(source, core, origin, second_send.at[source, hop], (other, mine))

    def third(source):
        origin = weights_out.at[source, core]
        return copy(source, core, origin, third_send.at[source], (me, twin))

    def arrived(source, index):
        origin = weights_out.at[source, index]
        copy(source, index, origin, third_send.at[source], (me, twin)).wait_recv()

    def loop(begin, end, body):
        def run(step, carry):
            body(step)
            return carry

        lax.fori_loop(begin, end, run, 0)

    def column_source(step):
        return lax.rem(row + rows - step, rows) * across + column

    loop(1, rows, lambda step: first(step).start())
    for hop in range(1, across):
        second(me, hop, weights.at[core]).start()
    moves[0][0]()
    moves[1][0]()
    moves[2][0]()

    def spread(step):
        source = column_source(step)
        arrived(source, core)
        for hop in range(1, across):
            second(source, hop, weights_out.at[source, core]).start()
        third(source).start()

    loop(1, rows, spread)

    def relay(step):
        for hop in range(1, across):
            source = lax.rem(row + rows - step, rows) * across + lax.rem(column + hop, across)
            arrived(source, core)
            third(source).start()

    loop(0, rows, relay)
    loop(1, shards, lambda step: arrived(lax.rem(me + step, shards), 1 - core))
    loop(1, rows, lambda step: first(step).wait_send())
    for hop in range(1, across):
        second(me, hop, weights.at[core]).wait_send()

    def drain(step):
        source = column_source(step)
        for hop in range(1, across):
            second(source, hop, weights_out.at[source, core]).wait_send()

    loop(1, rows, drain)
    loop(1, shards, lambda step: third(lax.rem(me + step, shards)).wait_send())
    own.wait()
    for _, finish in moves:
        finish()


def enter_call(shards, parts, tokens, cotangent, places, weights):
    count, length, model_width = tokens.shape
    width = count // parts
    whole = jax.ShapeDtypeStruct((width, length * parts, model_width), tokens.dtype)
    dma = pltpu.SemaphoreType.DMA
    return pl.pallas_call(
        functools.partial(enter_kernel, shards, parts, width, length),
        out_shape=[
            whole,
            whole,
            jax.ShapeDtypeStruct((1, parts) + places.shape[2:], places.dtype),
            jax.ShapeDtypeStruct((shards,) + weights.shape, weights.dtype),
        ],
        in_specs=[pl.BlockSpec(memory_space=pl.ANY)] * 4,
        out_specs=[pl.BlockSpec(memory_space=pl.ANY)] * 4,
        scratch_shapes=[
            dma((3, parts)),
            dma((3, parts)),
            dma((shards,)),
            dma((shards, parts)),
            dma((shards,)),
            dma((shards, 2)),
            dma,
        ],
        compiler_params=pltpu.CompilerParams(collective_id=0, has_side_effects=True),
        name="enter",
    )(tokens, cotangent, places, weights)


def leave_kernel(
    shards,
    parts,
    width,
    length,
    block_in,
    tokens_in,
    grads,
    block_out,
    tokens_out,
    summed,
    twin_in,
    column_send,
    column_in,
    row_send,
    row_in,
    chip_in,
    exchange_send,
    exchange_recv,
    twin_sends,
    twin_recvs,
    column_sends,
    column_recvs,
    row_sends,
    row_recvs,
    chip_sends,
    chip_recvs,
    last_send,
    last_recv,
):
    me, mine = lax.axis_index("fsdp"), lax.axis_index("ctx")
    chips = across = parts // 2
    rows = shards // across
    row, column = me // across, lax.rem(me, across)
    core = lax.rem(mine, 2)
    chip = mine // 2
    twin = chip * 2 + 1 - core
    greet(shards, parts, me, mine)
    moves = [
        exchange(
            source,
            target,
            width,
            length,
            parts,
            me,
            mine,
            exchange_send.at[index],
            exchange_recv.at[index],
            False,
        )
        for index, (source, target) in enumerate(((block_in, block_out), (tokens_in, tokens_out)))
    ]

    def loop(begin, end, body):
        def run(step, carry):
            body(step)
            return carry

        lax.fori_loop(begin, end, run, 0)

    def copy(source, target, send, recv, device):
        return pltpu.make_async_remote_copy(
            src_ref=source,
            dst_ref=target,
            send_sem=send,
            recv_sem=recv,
            device_id=device,
            device_id_type=MESH,
        )

    def to_twin(target):
        return copy(
            grads.at[target, 1 - core],
            twin_in.at[target],
            twin_sends.at[target],
            twin_recvs.at[target],
            (me, twin),
        )

    def along_row(line, other, slot):
        target = line * across + other
        return copy(
            column_send.at[target],
            column_in.at[line, slot],
            column_sends.at[target],
            column_recvs.at[line, slot],
            (row * across + other, mine),
        )

    def along_column(line, slot):
        return copy(
            row_send.at[line],
            row_in.at[slot],
            row_sends.at[line],
            row_recvs.at[slot],
            (line * across + column, mine),
        )

    def along_chips(hop, slot):
        other = lax.rem(chip + hop, chips)
        return copy(
            chip_in.at[chip],
            chip_in.at[slot],
            chip_sends.at[other],
            chip_recvs.at[slot],
            (me, other * 2 + core),
        )

    def line_of(step):
        return lax.rem(row + step, rows)

    def beside(hop):
        return lax.rem(column + hop, across)

    def wide(values):
        return values.astype(jnp.float32)

    def send_twin(step):
        for hop in range(1, across + 1):
            to_twin(line_of(step) * across + beside(hop)).start()

    loop(1, rows + 1, send_twin)
    for start, _ in moves:
        start()

    def send_column(step):
        line = line_of(step)
        for hop in range(1, across):
            target = line * across + beside(hop)
            to_twin(target).wait_recv()
            column_send[target] = (wide(grads[target, core]) + wide(twin_in[target])).astype(
                jnp.bfloat16
            )
            along_row(line, beside(hop), column).start()
        to_twin(line * across + column).wait_recv()

    loop(1, rows + 1, send_column)

    def send_row(line):
        target = line * across + column
        total = wide(grads[target, core]) + wide(twin_in[target])
        for hop in range(1, across):
            along_row(line, beside(hop), beside(hop)).wait_recv()
            total = total + wide(column_in[line, beside(hop)])
        row_send[line] = total.astype(jnp.bfloat16)

    def send_rows(step):
        line = line_of(step)
        send_row(line)
        along_column(line, row).start()

    loop(1, rows, send_rows)
    send_row(row)

    def add_row(step, total):
        line = lax.rem(row + rows - step, rows)
        along_column(line, line).wait_recv()
        return total + wide(row_in[line])

    chip_in[chip] = lax.fori_loop(1, rows, add_row, wide(row_send[row])).astype(jnp.bfloat16)
    for hop in range(1, chips):
        along_chips(hop, chip).start()
    for hop in range(1, chips):
        along_chips(hop, lax.rem(chip + hop, chips)).wait_recv()
    total = wide(chip_in[0])
    for index in range(1, chips):
        total = total + wide(chip_in[index])
    summed[core] = total.astype(jnp.bfloat16)
    copy(summed.at[core], summed.at[core], last_send, last_recv, (me, twin)).start()
    copy(summed.at[core], summed.at[1 - core], last_send, last_recv, (me, twin)).wait()
    for hop in range(1, chips):
        along_chips(hop, chip).wait_send()
    loop(1, rows, lambda step: along_column(line_of(step), row).wait_send())

    def drain(step):
        line = line_of(step)
        for hop in range(1, across):
            along_row(line, beside(hop), column).wait_send()
        for hop in range(1, across + 1):
            to_twin(line * across + beside(hop)).wait_send()

    loop(1, rows + 1, drain)
    for _, finish in moves:
        finish()


def leave_call(shards, parts, block_out, grad_tokens, grads):
    width, full_len, model_width = block_out.shape
    length = full_len // parts
    tile = grads.shape[2:]
    part = jax.ShapeDtypeStruct((width * parts, length, model_width), block_out.dtype)
    dma = pltpu.SemaphoreType.DMA
    across = parts // 2
    rows = shards // across
    any_space = pl.BlockSpec(memory_space=pl.ANY)
    on_chip = pl.BlockSpec(memory_space=pltpu.VMEM)
    return pl.pallas_call(
        functools.partial(leave_kernel, shards, parts, width, length),
        out_shape=[part, part, jax.ShapeDtypeStruct((2,) + tile, jnp.bfloat16)],
        in_specs=[any_space, any_space, on_chip],
        out_specs=[any_space, any_space, on_chip],
        scratch_shapes=[
            pltpu.VMEM((shards,) + tile, jnp.bfloat16),
            pltpu.VMEM((shards,) + tile, jnp.bfloat16),
            pltpu.VMEM((rows, across) + tile, jnp.bfloat16),
            pltpu.VMEM((rows,) + tile, jnp.bfloat16),
            pltpu.VMEM((rows,) + tile, jnp.bfloat16),
            pltpu.VMEM((across,) + tile, jnp.bfloat16),
            dma((2, parts)),
            dma((2, parts)),
            dma((shards,)),
            dma((shards,)),
            dma((shards,)),
            dma((rows, across)),
            dma((rows,)),
            dma((rows,)),
            dma((across,)),
            dma((across,)),
            dma,
            dma,
        ],
        compiler_params=pltpu.CompilerParams(
            collective_id=1, has_side_effects=True, vmem_limit_bytes=VMEM_LIMIT
        ),
        name="leave",
    )(block_out, grad_tokens, grads)


def local(
    tokens,
    segments,
    positions,
    query_weight,
    key_weight,
    value_weight,
    output_weight,
    gate_weight,
    up_weight,
    down_weight,
    attn_gain,
    ffn_gain,
    cotangent,
):
    shards, parts = lax.axis_size("fsdp"), lax.axis_size("ctx")
    own_rows = query_weight.shape[0]
    packed_rows = pack_rows(own_rows)
    wide = (
        query_weight,
        key_weight,
        value_weight,
        output_weight,
        gate_weight,
        up_weight,
        down_weight.reshape(own_rows, -1),
    )
    widths = [part.shape[1] for part in wide]
    pieces = split_columns(wide, 2)
    columns = pieces[0].shape[1]

    def with_gains(pieces, attn_row, ffn_row):
        lead = attn_row.shape[:-1]
        room = [(0, 0)] * len(lead)
        gains = jnp.stack([attn_row, ffn_row], axis=-2)
        gains = jnp.pad(
            gains, room + [(0, packed_rows - own_rows - 2), (0, columns - own_rows)]
        )
        return jnp.stack(
            [
                jnp.concatenate([piece, gains if index == 0 else jnp.zeros_like(gains)], axis=-2)
                for index, piece in enumerate(pieces)
            ],
            axis=-3,
        )

    count, local_len, _ = tokens.shape
    per_part = count // parts
    places = jnp.concatenate(
        [
            segments.reshape(parts, per_part, local_len),
            positions.reshape(parts, per_part, local_len),
        ],
        axis=1,
    )
    place_rows = -(-2 * per_part // 8) * 8
    places = jnp.pad(places, ((0, 0), (0, place_rows - 2 * per_part), (0, 0)))
    tokens, cotangent, places, gathered = enter_call(
        shards,
        parts,
        tokens,
        cotangent,
        places[:, None],
        with_gains(pieces, attn_gain, ffn_gain),
    )
    places = jnp.transpose(places[0], (1, 0, 2)).reshape(place_rows, -1)
    segments = places[:per_part]
    positions = places[per_part : 2 * per_part]
    full = join_columns([gathered[:, index, :own_rows] for index in range(2)], widths)
    full_query, full_key, full_value, full_output, full_gate, full_up = (
        part.reshape(shards * own_rows, -1) for part in full[:6]
    )
    full_down = full[6].reshape(-1, tokens.shape[2])
    full_attn = gathered[:, 0, own_rows, :own_rows].reshape(-1)
    full_ffn = gathered[:, 0, own_rows + 1, :own_rows].reshape(-1)
    seq_count, full_len, model_width = tokens.shape
    row_count = seq_count * full_len
    score_scale = 1.0 / math.sqrt(HEAD_DIM)
    attn_scale = full_attn.astype(jnp.float32)
    ffn_scale = full_ffn.astype(jnp.float32)
    inputs = tokens.astype(jnp.float32).reshape(row_count, model_width)
    scaled_one, inverse_one = normalize_parts(inputs)
    normed_one = (scaled_one * attn_scale).astype(jnp.bfloat16)
    def features(weight, rows):
        return lax.dot_general(
            weight, rows, (((0,), (1,)), ((), ())), preferred_element_type=jnp.float32
        )

    cosine, sine = tables(positions.reshape(row_count))
    queries = (rotate(features(full_query, normed_one), cosine, sine, HEADS) * score_scale).astype(
        jnp.bfloat16
    )
    key_rows = rotate(features(full_key, normed_one), cosine, sine, KV_HEADS).astype(jnp.bfloat16)
    value_rows = features(full_value, normed_one).astype(jnp.bfloat16)
    seg_row = segments.reshape(seq_count, 1, full_len)
    seg_column = segments.reshape(row_count, 1)
    mixed_rows, log_totals = attend(
        queries, key_rows, value_rows, seg_row, seg_column, seq_count, full_len
    )
    middle = inputs + dot_tn(mixed_rows, full_output)
    scaled_two, inverse_two = normalize_parts(middle)
    normed_two = (scaled_two * ffn_scale).astype(jnp.bfloat16)
    gate_pre = forward_dot(normed_two, full_gate)
    up_pre = forward_dot(normed_two, full_up)
    sigmoid_gate = jax.nn.sigmoid(gate_pre)
    silu_gate = gate_pre * sigmoid_gate
    hidden = (silu_gate * up_pre).astype(jnp.bfloat16)
    block_out = (middle + forward_dot(hidden, full_down)).astype(jnp.bfloat16).reshape(tokens.shape)
    grad_rows = cotangent.astype(jnp.float32).reshape(row_count, model_width)
    grad_low = grad_rows.astype(jnp.bfloat16)
    grad_down = contract_rows(hidden, grad_low)
    grad_hidden = times_transposed(grad_low, full_down)
    grad_up_in = (grad_hidden * silu_gate).astype(jnp.bfloat16)
    grad_gate_in = (
        grad_hidden * up_pre * sigmoid_gate * (1.0 + gate_pre * (1.0 - sigmoid_gate))
    ).astype(jnp.bfloat16)
    grad_gate = contract_rows(normed_two, grad_gate_in)
    grad_up = contract_rows(normed_two, grad_up_in)
    grad_normed_two = times_transposed(grad_gate_in, full_gate) + times_transposed(
        grad_up_in, full_up
    )
    grad_ffn = jnp.sum(grad_normed_two * scaled_two, axis=0)
    grad_middle = grad_rows + norm_back(grad_normed_two, scaled_two, inverse_two, ffn_scale)
    grad_branch = grad_middle.astype(jnp.bfloat16)
    grad_output = forward_dot(mixed_rows, grad_branch)
    grad_mixed = times_transposed(full_output, grad_branch).astype(jnp.bfloat16)
    grad_query_in, grad_key_in, grad_value_in = attend_back(
        queries,
        key_rows,
        value_rows,
        grad_mixed,
        mixed_rows,
        log_totals,
        seg_row,
        seg_column,
        cosine,
        sine,
        seq_count,
        full_len,
    )

    def weight_grad(grads):
        return lax.dot_general(
            normed_one, grads, (((0,), (1,)), ((), ())), preferred_element_type=jnp.float32
        )

    def row_grad(grads, weight):
        return lax.dot_general(
            grads, weight, (((0,), (1,)), ((), ())), preferred_element_type=jnp.float32
        )

    grad_query = weight_grad(grad_query_in)
    grad_key = weight_grad(grad_key_in)
    grad_value = weight_grad(grad_value_in)
    grad_normed_one = (
        row_grad(grad_query_in, full_query)
        + row_grad(grad_key_in, full_key)
        + row_grad(grad_value_in, full_value)
    )
    grad_attn = jnp.sum(grad_normed_one * scaled_one, axis=0)
    grad_tokens = (
        (grad_middle + norm_back(grad_normed_one, scaled_one, inverse_one, attn_scale))
        .astype(jnp.bfloat16)
        .reshape(tokens.shape)
    )
    grads = [
        grad.astype(jnp.bfloat16).reshape(shards, own_rows, -1)
        for grad in (
            grad_query,
            grad_key,
            grad_value,
            grad_output,
            grad_gate,
            grad_up,
            grad_down.astype(jnp.bfloat16),
        )
    ]
    packed = with_gains(
        split_columns(grads, 2),
        grad_attn.astype(jnp.bfloat16).reshape(shards, own_rows),
        grad_ffn.astype(jnp.bfloat16).reshape(shards, own_rows),
    )
    block_out, grad_tokens, summed = leave_call(shards, parts, block_out, grad_tokens, packed)
    summed = summed.astype(jnp.float32)
    owned = join_columns([summed[index, :own_rows] for index in range(2)], widths)
    owned[6] = owned[6].reshape(down_weight.shape)
    return (
        block_out,
        grad_tokens,
        *owned,
        summed[0, own_rows, :own_rows],
        summed[0, own_rows + 1, :own_rows],
    )


def solution(mesh):
    placed = (
        P("fsdp", "ctx", None),
        P("fsdp", "ctx"),
        P("fsdp", "ctx"),
        P("fsdp", None),
        P("fsdp", None),
        P("fsdp", None),
        P("fsdp", None),
        P("fsdp", None),
        P("fsdp", None),
        P("fsdp", None),
        P("fsdp"),
        P("fsdp"),
        P("fsdp", "ctx", None),
    )
    return jax.shard_map(
        local,
        mesh=mesh,
        in_specs=placed,
        out_specs=(
            P("fsdp", "ctx", None),
            P("fsdp", "ctx", None),
            P("fsdp", None),
            P("fsdp", None),
            P("fsdp", None),
            P("fsdp", None),
            P("fsdp", None),
            P("fsdp", None),
            P("fsdp", None),
            P("fsdp"),
            P("fsdp"),
        ),
        check_vma=False,
    )
```
